32 devices in a mesh: cuts: 8 (over z, x), row: 4 (over y, core).
Axes of the slice: x: 2, y: 2, z: 4, core: 2. Of those that a mesh axis runs over, the one named last changes fastest.
Arguments:
- operator: bfloat16 [8, 2404, 2404], P('cuts', 'row'), may hold values from -0.125 to 0.125
- incident: bfloat16 [8, 2404, 256], P('cuts', 'row'), may hold values from -6 to 6
- reflect: float32 [8, 3, 2404, 256], P('cuts', None, 'row'), may hold values from -0.8 to 0.8
- thickness_table: float32 [8], replicated, may hold values from 0.5 to 1.5
- profile: int32 [8], P('cuts'), may hold values from 0 to 7
- order_index: int32 [64], replicated, may hold values from 0 to 600
- cotangent: float32 [8, 64, 256], P('cuts'), may hold values from -6 to 6
Outputs:
- grad_operator: float32 [8, 2404, 2404], P('cuts', 'row')
- grad_incident: float32 [8, 2404, 256], P('cuts', 'row')
The draws below stay inside these ranges and needn't reach their ends.
All inputs are finite; a program needn't handle non-finite values.
Results may differ from the reference program's by a relative error of at most 0.0095.
Values may be sent and summed in bfloat16 or wider, within the bound.
No kernel may reach another device: no remote copies, remote signals or barrier semaphores. Data moves between devices by JAX's collectives and lax.ppermute only.
A program may use at most 128 MiB of HBM per device.

```python
import math
import jax
import jax.numpy as jnp
from jax import lax

ORDERS = 601
M = 2404
NB = 256
NSEL = 64
TAYLOR = 3
LEVELS = 3
PROFILES = 8
SLICES = 8


def with_ends(array, stream_key, least, high):
    shape = array.shape
    place = [jax.random.randint(jax.random.fold_in(stream_key, axis), (), 0, shape[axis]) for axis in range(len(shape))]
    array = array.at[tuple(place)].set(least)
    longest = shape.index(max(shape))
    place[longest] = (place[longest] + 1) % shape[longest]
    return array.at[tuple(place)].set(high)


def shard_levels(own_key, extent, cuts, least, high):
    level, own = 1.0, jax.random.fold_in(own_key, 6)
    for axis_at, blocks in cuts:
        heights = jnp.exp(jax.random.uniform(jax.random.fold_in(own, axis_at), (blocks,), jnp.float32, least / len(cuts), high / len(cuts)))
        level = level * jnp.repeat(heights, extent[axis_at] // blocks).reshape([-1 if axis == axis_at else 1 for axis in range(len(extent))])
    return level


def centred(stream_key, shape, spread, limit, cuts=(), dtype=jnp.bfloat16):
    loudness = shard_levels(stream_key, shape, cuts, -0.22, 0.18) if cuts else 1.0
    result = jax.random.normal(stream_key, shape, jnp.float32) * spread * loudness
    return jnp.minimum(jnp.maximum(result, -limit), limit).astype(dtype)


def setup_inputs(seed: int = 0) -> dict:
    arg_keys = jax.random.split(jax.random.key(seed), 8)
    operator = centred(arg_keys[0], (SLICES, M, M), M ** -0.5, 0.125, ((0, 8), (1, 4)))
    incident = centred(arg_keys[1], (SLICES, M, NB), 1.0, 6.0, ((0, 8), (1, 4)))
    reflect = jnp.clip(jax.random.uniform(arg_keys[2], (SLICES, LEVELS, M, NB), jnp.float32, -0.8, 0.8) * shard_levels(arg_keys[2], (SLICES, LEVELS, M, NB), ((0, 8), (2, 4)), -0.4, 0.0), -0.8, 0.8)
    thickness_table = jnp.clip(jnp.exp(jax.random.uniform(arg_keys[3], (PROFILES,), jnp.float32, math.log(0.5), math.log(1.5))), 0.5, 1.5)
    profile = with_ends(jax.random.randint(arg_keys[4], (SLICES,), 0, PROFILES), jax.random.fold_in(arg_keys[4], 1), 0, PROFILES - 1).astype(jnp.int32)
    order_index = with_ends(jax.random.randint(arg_keys[5], (NSEL,), 0, ORDERS), jax.random.fold_in(arg_keys[5], 1), 0, ORDERS - 1).astype(jnp.int32)
    cotangent = centred(arg_keys[6], (SLICES, NSEL, NB), 1.0, 6.0, ((0, 8),), jnp.float32)
    return dict(operator=operator, incident=incident, reflect=reflect, thickness_table=thickness_table, profile=profile, order_index=order_index, cotangent=cotangent)


def taylor_forward(a_matrix, x_input, step_len):
    current = x_input
    x_wide = x_input.astype(jnp.float32)
    stored = []
    for degree in range(TAYLOR, 0, -1):
        stored.append(current)
        product = jnp.dot(a_matrix, current, preferred_element_type=jnp.float32)
        current = (x_wide + step_len / degree * product).astype(jnp.bfloat16)
    return (current, jnp.stack(stored))

def taylor_backward(a_matrix, stored, upstream, step_len):
    grad_input = jnp.zeros(upstream.shape, jnp.float32)
    grad_matrix = jnp.zeros(a_matrix.shape, jnp.float32)
    for degree in range(1, TAYLOR + 1):
        grad_input = grad_input + upstream
        scaled = (step_len / degree * upstream).astype(jnp.bfloat16)
        iterate = stored[TAYLOR - degree]
        grad_matrix = grad_matrix + jnp.dot(scaled, iterate.T, preferred_element_type=jnp.float32)
        upstream = jnp.dot(a_matrix.T, scaled, preferred_element_type=jnp.float32)
    grad_input = grad_input + upstream
    return (grad_matrix, grad_input)

def reference(operator, incident, reflect, thickness_table, profile, order_index, cotangent):
    step_all = lax.optimization_barrier(jnp.sum(jnp.where(profile[:, None] == jnp.arange(PROFILES)[None, :], thickness_table[None, :], 0.0), axis=1))

    def forward_one(packed):
        return taylor_forward(packed[0], packed[1], packed[2])
    fields, stored = lax.map(forward_one, (operator, incident, step_all))
    merged = fields.astype(jnp.float32)
    slice_index = jnp.arange(SLICES)
    for section_level in range(LEVELS):
        partner = jnp.bitwise_xor(slice_index, 1 << section_level)
        merged = merged + reflect[partner, section_level] * merged[partner]
    order_of = jnp.arange(M) % ORDERS
    onehot = (order_of[:, None] == order_index[None, :]).astype(jnp.float32)
    cmap = jnp.einsum('ij,sjn->sin', onehot, cotangent, precision=lax.Precision.HIGHEST)
    squared = merged * merged
    power = lax.optimization_barrier(jnp.sum(squared, axis=1))
    weighted = lax.optimization_barrier(jnp.sum(cmap * squared, axis=1))
    mean_power = power / M + 1e-06
    scale = 1.0 / math.sqrt(NB)
    grad_field = scale * (2.0 * cmap * merged / mean_power[:, None, :] - 2.0 / M * (weighted / (mean_power * mean_power))[:, None, :] * merged)
    for section_level in range(LEVELS - 1, -1, -1):
        partner = jnp.bitwise_xor(slice_index, 1 << section_level)
        grad_field = grad_field + reflect[:, section_level] * grad_field[partner]

    def backward_one(packed):
        return taylor_backward(packed[0], packed[1], packed[2], packed[3])
    grad_operator, grad_incident = lax.map(backward_one, (operator, stored, grad_field, step_all))
    return (grad_operator, grad_incident)
```

```python
import functools
import math

import jax
import jax.numpy as jnp
from jax import lax
from jax.experimental import pallas as pl
from jax.experimental.pallas import tpu as pltpu
from jax.sharding import PartitionSpec as P

ORDERS = 601
TAYLOR = 3
LEVELS = 3
CHUNKS = 1
LANES = 128
F32 = jnp.float32
BF16 = jnp.bfloat16
WHOLE = pl.BlockSpec(memory_space=pltpu.VMEM)
SCALAR = pl.BlockSpec(memory_space=pltpu.SMEM)


def call(body, out_shape, in_specs, scratch=(), limit=48):
    out_specs = jax.tree.map(lambda _: WHOLE, out_shape)
    return pl.pallas_call(
        body,
        out_shape=out_shape,
        in_specs=in_specs,
        out_specs=out_specs,
        scratch_shapes=list(scratch),
        compiler_params=pltpu.CompilerParams(vmem_limit_bytes=limit * 2**20),
    )


def over_row(value, mask):
    pairs = [(source, source ^ mask) for source in range(lax.axis_size("row"))]
    return lax.ppermute(value, "row", pairs)


def over_cuts(value):
    size = lax.axis_size("cuts")
    group = 2**LEVELS
    groups = None
    if size != group:
        groups = [list(range(first, first + group)) for first in range(0, size, group)]
    return lax.all_to_all(value, "cuts", 0, 0, axis_index_groups=groups, tiled=True)


def operator_blocks(me_ref, a_ref, out_ref):
    rows, full = a_ref.shape
    out_ref[...] = jnp.zeros_like(out_ref)
    for block in range(full // rows):
        out_ref[me_ref[0] ^ block, :rows, :rows] = a_ref[:, block * rows : (block + 1) * rows]


def turned(x_ref, out_ref, tall):
    rows = x_ref.shape[0]
    tall[rows:, :] = jnp.zeros_like(tall[rows:, :])
    tall[:rows, :] = x_ref[...].astype(F32)
    out_ref[...] = tall[...].T.astype(BF16)


def coupling(chunks, reflect_ref, cotangent_ref, out_ref, tall):
    levels, rows, columns = reflect_ref.shape
    pad = tall.shape[0]
    group = 2**levels
    part = columns // chunks // group
    tall[rows:, :] = jnp.zeros_like(tall[rows:, :])
    cot = cotangent_ref[...].T
    high = cot.astype(BF16)
    low = (cot - high.astype(F32)).astype(BF16)
    tracked = cot.shape[1]
    for piece, first in [(high, levels * pad), (low, levels * pad + tracked)]:
        for chunk in range(chunks):
            for peer in range(group):
                at = (chunk * group + peer) * part
                out_ref[peer, chunk, :, first : first + tracked] = piece[at : at + part]
    for level in range(levels):
        tall[:rows, :] = reflect_ref[level]
        flat = tall[...].T.astype(BF16)
        for chunk in range(chunks):
            for peer in range(group):
                at = (chunk * group + peer) * part
                out_ref[peer, chunk, :, level * pad : (level + 1) * pad] = flat[at : at + part]


def merge(levels, w_ref, rc_ref, onehot_ref, field_ref, cmap_ref, sums_ref):
    group, part, pad = w_ref.shape
    totals = []
    merged = [w_ref[s].astype(F32) for s in range(group)]
    for level in range(levels):
        sent = [
            rc_ref[s, :, level * pad : (level + 1) * pad].astype(F32) * merged[s] for s in range(group)
        ]
        merged = [merged[s] + sent[s ^ 2**level] for s in range(group)]
    lane = lax.broadcasted_iota(jnp.int32, (part, LANES), 1)
    for s in range(group):
        field = merged[s]
        cmap = jnp.dot(rc_ref[s, :, levels * pad :], onehot_ref[...], preferred_element_type=F32)
        squared = field * field
        power = jnp.sum(squared, axis=1, keepdims=True)
        weighted = jnp.sum(cmap * squared, axis=1, keepdims=True)
        field_ref[s] = field
        cmap_ref[s] = cmap
        totals.append(jnp.where(lane == 0, power, jnp.where(lane == 1, weighted, 0.0)))
    sums_ref[...] = jnp.concatenate(totals, axis=0).T[: sums_ref.shape[0]]


def unmerge(levels, full, scale, field_ref, cmap_ref, rc_ref, s0, s1, s2, s3, out_ref):
    group, part, pad = field_ref.shape
    sums = (s0[...] + s1[...]) + (s2[...] + s3[...])
    sums = jnp.concatenate([sums] * (LANES // sums.shape[0]), axis=0).T
    grad = []
    for s in range(group):
        power = sums[s * part : (s + 1) * part, 0:1]
        weighted = sums[s * part : (s + 1) * part, 1:2]
        inverse = 1.0 / (power / full + 1e-06)
        first = scale * 2.0 * inverse
        second = scale * 2.0 / full * (weighted * inverse * inverse)
        grad.append((first * cmap_ref[s] - second) * field_ref[s])
    for level in range(levels - 1, -1, -1):
        grad = [
            grad[s]
            + rc_ref[s, :, level * pad : (level + 1) * pad].astype(F32) * grad[s ^ 2**level]
            for s in range(group)
        ]
    for s in range(group):
        out_ref[s] = grad[s].astype(BF16)


def shape(*dims, dtype=F32):
    return jax.ShapeDtypeStruct(dims, dtype)


def times_t(block, panel):
    return lax.dot_general(block, panel, (((1,), (1,)), ((), ())), preferred_element_type=F32)


def times(block, panel):
    return lax.dot_general(block, panel, (((1,), (0,)), ((), ())), preferred_element_type=F32)


def local(operator, incident, reflect, thickness_table, profile, order_index, cotangent):
    rows, full = operator.shape[1:]
    columns = incident.shape[2]
    levels = reflect.shape[1]
    group = 2**levels
    tracked = order_index.shape[0]
    pad = -(-rows // LANES) * LANES
    width = columns // CHUNKS
    part = width // group
    me = lax.axis_index("row")
    me_arr = me.reshape(1)
    step_len = jnp.sum(jnp.where(profile[0] == jnp.arange(thickness_table.shape[0]), thickness_table, 0.0))

    x_t = call(turned, shape(columns, pad, dtype=BF16), [WHOLE], [pltpu.VMEM((pad, columns), F32)])(incident[0])
    rc = call(
        functools.partial(coupling, CHUNKS),
        shape(group, CHUNKS, part, levels * pad + 2 * tracked, dtype=BF16),
        [WHOLE, WHOLE],
        [pltpu.VMEM((pad, columns), F32)],
    )(reflect[0], cotangent[0])
    rc = over_cuts(rc)
    panel = call(operator_blocks, shape(4, pad, pad, dtype=BF16), [SCALAR, WHOLE])(me_arr, operator[0])

    lane_row = jnp.arange(pad, dtype=jnp.int32)
    lane_order = jnp.where(lane_row < rows, (me * rows + lane_row) % ORDERS, -1)
    tracked_twice = jnp.concatenate([order_index, order_index])
    onehot = (tracked_twice[:, None] == lane_order[None, :]).astype(BF16)

    outs = []
    for chunk in range(CHUNKS):
        x = x_t[chunk * width : (chunk + 1) * width]
        x_wide = x.astype(F32)
        current = x
        stored = []
        for degree in range(TAYLOR, 0, -1):
            far = over_row(current, 2)
            core = over_row(current, 1)
            product = times_t(current, panel[0]) + times_t(core, panel[1])
            diag = over_row(far, 1)
            product = product + times_t(far, panel[2])
            product = product + times_t(diag, panel[3])
            stored.append((current, core, far, diag))
            current = (x_wide + step_len / degree * product).astype(BF16)
        swapped = over_cuts(current.reshape(group, part, pad))
        coupled = rc[:, chunk]
        field, cmap, sums = call(
            functools.partial(merge, levels),
            (shape(group, part, pad), shape(group, part, pad), shape(8, group * part)),
            [WHOLE] * 3,
        )(swapped, coupled, onehot)
        s1, s2, s3 = (over_row(sums, mask) for mask in (1, 2, 3))
        grad = call(
            functools.partial(unmerge, levels, full, 1.0 / math.sqrt(columns)),
            shape(group, part, pad, dtype=BF16),
            [WHOLE] * 7,
        )(field, cmap, coupled, sums, s1, s2, s3)
        upstream = over_cuts(grad).reshape(width, pad).astype(F32)
        total = jnp.zeros((width, pad), F32)
        scaled_all = []
        for degree in range(1, TAYLOR + 1):
            total = total + upstream
            scaled = (step_len / degree * upstream).astype(BF16)
            scaled_all.append(scaled)
            diag = over_row(times(scaled, panel[3]).astype(BF16), 1)
            far = times(scaled, panel[2])
            far = over_row((far + diag.astype(F32)).astype(BF16), 2)
            core = over_row(times(scaled, panel[1]).astype(BF16), 1)
            upstream = times(scaled, panel[0]) + core.astype(F32) + far.astype(F32)
        total = total + upstream
        outs.append((total, stored, scaled_all))
    grad_incident = jnp.concatenate([out[0][:, :rows] for out in outs], axis=0).T

    left = jnp.concatenate([scaled for out in outs for scaled in out[2]], axis=0)[:, :rows]
    blocks = []
    for block in range(4):
        pieces = []
        for out in outs:
            for stored in out[1][::-1]:
                pieces.append(lax.dynamic_index_in_dim(jnp.stack(stored), me ^ block, 0, keepdims=False))
        blocks.append(jnp.concatenate(pieces, axis=0)[:, :rows])
    right = jnp.concatenate(blocks, axis=1)
    grad_matrix = lax.dot_general(left, right, (((0,), (0,)), ((), ())), preferred_element_type=F32)
    return (grad_matrix[None], grad_incident[None])


def solution(mesh):
    return jax.shard_map(
        local,
        mesh=mesh,
        in_specs=(
            P("cuts", "row", None),
            P("cuts", "row", None),
            P("cuts", None, "row", None),
            P(),
            P("cuts"),
            P(),
            P("cuts", None, None),
        ),
        out_specs=(P("cuts", "row", None), P("cuts", "row", None)),
        check_vma=False,
    )
```

```python
import functools
import math

import jax
import jax.numpy as jnp
from jax import lax
from jax.experimental import pallas as pl
from jax.experimental.pallas import tpu as pltpu
from jax.sharding import PartitionSpec as P

ORDERS = 601
TAYLOR = 3
LEVELS = 3
SPLIT = (128, 128)
CHUNKS = len(SPLIT)
LANES = 128
HALVES = 2
F32 = jnp.float32
BF16 = jnp.bfloat16
WHOLE = pl.BlockSpec(memory_space=pltpu.VMEM)
SCALAR = pl.BlockSpec(memory_space=pltpu.SMEM)


def shape(*dims, dtype=F32):
    return jax.ShapeDtypeStruct(dims, dtype)


def call(body, out_shape, *args, scratch=(), limit=8):
    return pl.pallas_call(
        body,
        out_shape=out_shape,
        in_specs=[SCALAR if arg.size <= 8 else WHOLE for arg in args],
        out_specs=jax.tree.map(lambda _: WHOLE, out_shape),
        scratch_shapes=list(scratch),
        compiler_params=pltpu.CompilerParams(vmem_limit_bytes=limit * 2**20),
        cost_estimate=pl.CostEstimate(flops=0, transcendentals=0, bytes_accessed=1),
    )(*args)


def split(refs, value):
    first = 0
    for ref in refs:
        ref[...] = value[first : first + ref.shape[0]]
        first += ref.shape[0]


def joined(refs):
    return jnp.concatenate([ref[...] for ref in refs], axis=0)


def after(value, token):
    return lax.optimization_barrier((value, token))[0]


def over_row(value, mask):
    pairs = [(source, source ^ mask) for source in range(lax.axis_size("row"))]
    return lax.ppermute(value, "row", pairs)


def over_cuts(value):
    size = lax.axis_size("cuts")
    group = 2**LEVELS
    groups = None
    if size != group:
        groups = [list(range(first, first + group)) for first in range(0, size, group)]
    return lax.all_to_all(value, "cuts", 0, 0, axis_index_groups=groups, tiled=True)


def times_t(block, panel):
    return lax.dot_general(block, panel, (((1,), (1,)), ((), ())), preferred_element_type=F32)


def times(block, panel):
    return lax.dot_general(block, panel, (((1,), (0,)), ((), ())), preferred_element_type=F32)


def operator_blocks(me_ref, profile_ref, table_ref, a_ref, out_ref, step_ref):
    rows, full = a_ref.shape
    pad = out_ref.shape[1]
    step_ref[...] = jnp.full(step_ref.shape, table_ref[profile_ref[0]], F32)
    for block in range(full // rows):
        place = me_ref[0] ^ block
        out_ref[place, rows // 16 * 16 :, :] = jnp.zeros((pad - rows // 16 * 16, pad), BF16)
        out_ref[place, :, rows // LANES * LANES :] = jnp.zeros((pad, pad - rows // LANES * LANES), BF16)
        out_ref[place, :rows, :rows] = a_ref[:, block * rows : (block + 1) * rows]


def turned(me_ref, x_ref, *refs):
    tall = refs[-1]
    rows = x_ref.shape[0]
    tall[rows:, :] = jnp.zeros_like(tall[rows:, :])
    tall[:rows, :] = x_ref[...].astype(F32)
    flat = tall[...].T.astype(BF16)
    first = 0
    for out_ref in refs[:-1]:
        out_ref[...] = flat[first : first + out_ref.shape[0]]
        first += out_ref.shape[0]


def coupling(reflect_ref, cotangent_ref, out_ref, tall):
    levels, rows, _, columns = reflect_ref.shape
    pad = tall.shape[0]
    group, part = out_ref.shape[:2]
    tall[rows:, :] = jnp.zeros_like(tall[rows:, :])
    cot = cotangent_ref[...].T
    high = cot.astype(BF16)
    low = (cot - high.astype(F32)).astype(BF16)
    tracked = cot.shape[1]
    first = levels * pad
    out_ref[:, :, first : first + tracked] = high.reshape(group, part, tracked)
    out_ref[:, :, first + tracked :] = low.reshape(group, part, tracked)
    for level in range(levels):
        tall[:rows, :] = reflect_ref[level, :, 0, :]
        out_ref[:, :, level * pad : (level + 1) * pad] = tall[...].T.astype(BF16).reshape(group, part, pad)


def forward_near(own_ref, core_ref, panel_ref, out_ref, *copies):
    out_ref[...] = times_t(own_ref[...], panel_ref[0]) + times_t(core_ref[...], panel_ref[1])
    for copy_ref in copies:
        copy_ref[...] = own_ref[...]


def forward_far(near_ref, far_ref, panel_ref, out_ref, *halves):
    out_ref[...] = near_ref[...] + times_t(far_ref[...], panel_ref[2])
    split(halves, far_ref[...])


def forward_last(degree, step_ref, x_ref, most_ref, panel_ref, *refs):
    product = most_ref[...] + times_t(joined(refs[:HALVES]), panel_ref[3])
    value = (x_ref[...].astype(F32) + step_ref[0:1, 0:1] / degree * product).astype(BF16)
    out_ref = refs[-1]
    first = 0
    for ref in refs[HALVES:-1]:
        out_ref[first : first + ref.shape[0]] = ref[...]
        first += ref.shape[0]
    out_ref[first:] = value


def merge(levels, rows, me_ref, order_ref, w_ref, rc_ref, field_ref, cmap_ref, level_ref, sums_ref):
    group, part, pad = w_ref.shape
    tracked = order_ref.shape[1]
    tail = level_ref.shape[2]
    place = lax.broadcasted_iota(jnp.int32, (pad, tracked), 0)
    order = jnp.where(place < rows, (place + me_ref[0] * rows) % ORDERS, -1)
    onehot = jnp.where(order == order_ref[...], 1.0, 0.0).astype(BF16)
    onehot = jnp.concatenate([onehot, onehot], axis=1)
    totals = []
    merged = [w_ref[s].astype(F32) for s in range(group)]
    level_ref[...] = rc_ref[:, :, :tail]
    for level in range(levels):
        sent = [
            rc_ref[s, :, level * pad : (level + 1) * pad].astype(F32) * merged[s] for s in range(group)
        ]
        merged = [merged[s] + sent[s ^ 2**level] for s in range(group)]
    lane = lax.broadcasted_iota(jnp.int32, (part, LANES), 1)
    for s in range(group):
        field = merged[s]
        cmap = times_t(rc_ref[s, :, tail:], onehot)
        squared = field * field
        power = jnp.sum(squared, axis=1, keepdims=True)
        weighted = jnp.sum(cmap * squared, axis=1, keepdims=True)
        field_ref[s] = field
        cmap_ref[s] = cmap
        totals.append(jnp.where(lane == 0, power, jnp.where(lane == 1, weighted, 0.0)))
    sums_ref[...] = jnp.concatenate(totals, axis=0).T[: sums_ref.shape[0]]


def unmerge(levels, full, scale, field_ref, cmap_ref, rc_ref, s0, s1, s2, s3, out_ref):
    group, part, pad = field_ref.shape
    sums = (s0[...] + s1[...]) + (s2[...] + s3[...])
    sums = jnp.concatenate([sums] * (LANES // sums.shape[0]), axis=0).T
    grad = []
    for s in range(group):
        power = sums[s * part : (s + 1) * part, 0:1]
        weighted = sums[s * part : (s + 1) * part, 1:2]
        inverse = 1.0 / (power / full + 1e-06)
        first = scale * 2.0 * inverse
        second = scale * 2.0 / full * (weighted * inverse * inverse)
        grad.append((first * cmap_ref[s] - second) * field_ref[s])
    for level in range(levels - 1, -1, -1):
        grad = [
            grad[s]
            + rc_ref[s, :, level * pad : (level + 1) * pad].astype(F32) * grad[s ^ 2**level]
            for s in range(group)
        ]
    for s in range(group):
        out_ref[s] = grad[s].astype(BF16)


def columns_of(me_ref, *refs):
    out_ref, pile = refs[-2:]
    places = pile.shape[0]
    rows = out_ref.shape[1] // places
    first = 0
    each = places - 1 + HALVES
    for chunk in range((len(refs) - 2) // each):
        group = refs[chunk * each : (chunk + 1) * each]
        width = group[0].shape[0]
        for place in range(places - 1):
            pile[me_ref[0] ^ place, first : first + width, :] = group[place][...]
        pile[me_ref[0] ^ (places - 1), first : first + width, :] = joined(group[places - 1 :])
        first += width
    for block in range(places):
        out_ref[:, block * rows : (block + 1) * rows] = pile[block, :, :rows]


def backward_first(first, step_ref, whole_ref, panel_ref, scaled_ref, total_ref, *refs):
    width = scaled_ref.shape[0]
    upstream = whole_ref[first : first + width]
    for ref in refs[HALVES:]:
        ref[...] = whole_ref[width:]
    total_ref[...] = upstream.astype(F32)
    scaled = (step_ref[0:1, 0:1] * upstream.astype(F32)).astype(BF16)
    scaled_ref[...] = scaled
    split(refs[:HALVES], times(scaled, panel_ref[3]).astype(BF16))


def backward_next(degree, step_ref, near_ref, core_ref, far_ref, before_ref, panel_ref, scaled_ref, total_ref, *sent):
    upstream = near_ref[...] + core_ref[...].astype(F32) + far_ref[...].astype(F32)
    total_ref[...] = before_ref[...] + upstream
    scaled = (step_ref[0:1, 0:1] / degree * upstream).astype(BF16)
    scaled_ref[...] = scaled
    split(sent, times(scaled, panel_ref[3]).astype(BF16))


def backward_far(scaled_ref, panel_ref, *refs):
    product = times(scaled_ref[...], panel_ref[2])
    refs[-1][...] = (product + joined(refs[:-1]).astype(F32)).astype(BF16)


def backward_near(scaled_ref, panel_ref, sent_ref, near_ref):
    sent_ref[...] = times(scaled_ref[...], panel_ref[1]).astype(BF16)
    near_ref[...] = times(scaled_ref[...], panel_ref[0])


def outer(chunks, *refs):
    out_ref = refs[-1]
    rights = refs[-1 - TAYLOR : -1]
    total = None
    for degree, right in enumerate(rights):
        left = jnp.concatenate([ref[...] for ref in refs[degree * chunks : (degree + 1) * chunks]], axis=0)
        value = lax.dot_general(left, right[...], (((0,), (0,)), ((), ())), preferred_element_type=F32)
        total = value if total is None else total + value
    out_ref[:, 0, :] = total


def finish(*refs):
    out_ref = refs[-1]
    rows = out_ref.shape[0]
    values = []
    for chunk in range(len(refs) // 4):
        near, total, core, far = (ref[...].astype(F32) for ref in refs[4 * chunk : 4 * chunk + 4])
        values.append((near + total) + (core + far))
    value = jnp.concatenate(values, axis=0).T
    out_ref[:, 0, :] = value[:rows]


def local(operator, incident, reflect, thickness_table, profile, order_index, cotangent):
    rows, full = operator.shape[1:]
    columns = incident.shape[2]
    levels = reflect.shape[1]
    group = 2**levels
    tracked = order_index.shape[0]
    pad = -(-rows // LANES) * LANES
    part = columns // group
    count = range(CHUNKS)
    me = lax.axis_index("row")
    me_arr = me.reshape(1)
    widths = [columns * share // sum(SPLIT) for share in SPLIT]
    blocks = [shape(width, pad, dtype=BF16) for width in widths]
    wides = [shape(width, pad) for width in widths]
    parts = [[shape(width // HALVES, pad, dtype=BF16)] * HALVES for width in widths]

    rc = call(
        coupling,
        shape(group, part, levels * pad + 2 * tracked, dtype=BF16),
        reflect.transpose(1, 2, 0, 3),
        cotangent[0],
        scratch=[pltpu.VMEM((pad, columns), F32)],
        limit=10,
    )
    x = call(turned, blocks, after(me_arr, rc), incident[0], scratch=[pltpu.VMEM((pad, columns), F32)])
    rc = over_cuts(rc)
    fars = [over_row(value, 2) for value in x]
    cores = [over_row(value, 1) for value in x]
    panel, step = call(
        operator_blocks,
        (shape(4, pad, pad, dtype=BF16), shape(8, LANES)),
        after(me_arr, x[0]), profile, thickness_table, operator[0],
        limit=12,
    )
    token = panel

    current = list(x)
    stored = [[] for _ in count]
    rights = []
    x = list(x)

    def write_columns(place, pieces):
        return call(
            columns_of,
            shape(columns, full, dtype=BF16),
            place, *pieces,
            scratch=[pltpu.VMEM((4, columns, pad), BF16)],
            limit=6,
        )

    for degree in range(TAYLOR, 0, -1):
        next_fars, next_cores = [], []
        for chunk in count:
            near = call(
                forward_near,
                [wides[chunk]] + [blocks[chunk]] * (degree == TAYLOR),
                current[chunk], after(cores[chunk], token), panel,
            )
            if degree == TAYLOR:
                x[chunk] = near[1]
            far = after(fars[chunk], near[0])
            most, *halves = call(
                forward_far, [wides[chunk]] + parts[chunk], near[0], far, panel
            )
            diag = [over_row(half, 1) for half in halves]
            stored[chunk].append((current[chunk], cores[chunk], far, *diag))
            final = degree == 1 and chunk == CHUNKS - 1
            value = call(
                functools.partial(forward_last, degree),
                shape(columns, pad, dtype=BF16) if final else blocks[chunk],
                step, x[chunk], most, panel, *diag,
                *(current[:-1] if final else []),
            )
            current[chunk] = value
            token = value
            if degree > 1:
                next_fars.append(over_row(value, 2))
                next_cores.append(over_row(value, 1))
        fars, cores = next_fars, next_cores
        pieces = [piece for chunk in count for piece in stored[chunk][-1]]
        place = after(me_arr, token)
        if degree > 1:
            token = write_columns(place, pieces)
            rights.append(token)

    current[-1], rc = lax.optimization_barrier((current[-1], rc))
    swapped = over_cuts(current[-1].reshape(group, part, pad))
    field, cmap, coupled, sums = call(
        functools.partial(merge, levels, rows),
        (
            shape(group, part, pad),
            shape(group, part, pad),
            shape(group, part, levels * pad, dtype=BF16),
            shape(8, group * part),
        ),
        me_arr, order_index.reshape(1, tracked), swapped, rc,
        limit=12,
    )
    s1, s2, s3 = (over_row(sums, mask) for mask in (1, 2, 3))
    grad = call(
        functools.partial(unmerge, levels, full, 1.0 / math.sqrt(columns)),
        shape(group, part, pad, dtype=BF16),
        field, cmap, coupled, sums, s1, s2, s3,
    )
    whole = over_cuts(grad).reshape(columns, pad)
    token = write_columns(after(place, grad), pieces)
    rights.append(token)

    total = [None] * CHUNKS
    pending = [None] * CHUNKS
    scaled_all = []
    for degree in range(1, TAYLOR + 1):
        for chunk in count:
            outs = [blocks[chunk], wides[chunk]] + parts[chunk]
            if degree == 1:
                scaled, total[chunk], *sent = call(
                    functools.partial(backward_first, 0),
                    outs + ([blocks[1]] if chunk == 0 and CHUNKS == 2 else []),
                    step, after(whole, token), panel,
                )
                if chunk == 0 and CHUNKS == 2:
                    whole = sent.pop()
            else:
                near, core, far = pending[chunk]
                scaled, total[chunk], *sent = call(
                    functools.partial(backward_next, degree), outs,
                    step, near, core, after(far, token), total[chunk], panel,
                )
            scaled_all.append(scaled)
            diag = [over_row(half, 1) for half in sent]
            sent = call(backward_far, blocks[chunk], scaled, panel, *diag)
            far = over_row(sent, 2)
            sent, near = call(backward_near, (blocks[chunk], wides[chunk]), after(scaled, sent), panel)
            core = over_row(sent, 1)
            token = near
            pending[chunk] = (near, core, far)
    grad_matrix = pl.pallas_call(
        functools.partial(outer, CHUNKS),
        grid=(pad // LANES,),
        out_shape=shape(rows, 1, full),
        in_specs=[pl.BlockSpec((scaled.shape[0], LANES), lambda i: (0, i)) for scaled in scaled_all]
        + [WHOLE] * TAYLOR,
        out_specs=pl.BlockSpec((LANES, 1, full), lambda i: (i, 0, 0)),
        compiler_params=pltpu.CompilerParams(vmem_limit_bytes=20 * 2**20),
        cost_estimate=pl.CostEstimate(flops=0, transcendentals=0, bytes_accessed=1),
    )(*scaled_all[:-1], after(scaled_all[-1], token), *rights[::-1])
    args = []
    for chunk in count:
        near, core, far = pending[chunk]
        args += [near, total[chunk], core, far]
    args[-1] = after(args[-1], grad_matrix)
    grad_incident = call(finish, shape(rows, 1, columns), *args)
    return (grad_matrix.transpose(1, 0, 2), grad_incident.transpose(1, 0, 2))


def solution(mesh):
    return jax.shard_map(
        local,
        mesh=mesh,
        in_specs=(
            P("cuts", "row", None),
            P("cuts", "row", None),
            P("cuts", None, "row", None),
            P(),
            P("cuts"),
            P(),
            P("cuts", None, None),
        ),
        out_specs=(P("cuts", "row", None), P("cuts", "row", None)),
        check_vma=False,
    )
```

```python
import functools
import math

import jax
import jax.numpy as jnp
from jax import lax
from jax.experimental import pallas as pl
from jax.experimental.pallas import tpu as pltpu
from jax.sharding import PartitionSpec as P

ORDERS = 601
TAYLOR = 3
LEVELS = 3
SPLIT = (128, 128)
CHUNKS = len(SPLIT)
LANES = 128
COST = 5000000000
HALVES = 2
F32 = jnp.float32
BF16 = jnp.bfloat16
WHOLE = pl.BlockSpec(memory_space=pltpu.VMEM)
SCALAR = pl.BlockSpec(memory_space=pltpu.SMEM)


def shape(*dims, dtype=F32):
    return jax.ShapeDtypeStruct(dims, dtype)


def call(body, out_shape, *args, scratch=(), limit=8):
    return pl.pallas_call(
        body,
        out_shape=out_shape,
        in_specs=[SCALAR if arg.size <= 8 else WHOLE for arg in args],
        out_specs=jax.tree.map(lambda _: WHOLE, out_shape),
        scratch_shapes=list(scratch),
        compiler_params=pltpu.CompilerParams(vmem_limit_bytes=limit * 2**20),
        cost_estimate=pl.CostEstimate(flops=0, transcendentals=0, bytes_accessed=1),
    )(*args)


def split(refs, value):
    first = 0
    for ref in refs:
        ref[...] = value[first : first + ref.shape[0]]
        first += ref.shape[0]


def joined(refs):
    return jnp.concatenate([ref[...] for ref in refs], axis=0)


def after(value, token):
    return lax.optimization_barrier((value, token))[0]


def over_row(value, mask):
    pairs = [(source, source ^ mask) for source in range(lax.axis_size("row"))]
    return lax.ppermute(value, "row", pairs)


def over_cuts(value):
    size = lax.axis_size("cuts")
    group = 2**LEVELS
    groups = None
    if size != group:
        groups = [list(range(first, first + group)) for first in range(0, size, group)]
    return lax.all_to_all(value, "cuts", 0, 0, axis_index_groups=groups, tiled=True)


def times_t(block, panel):
    return lax.dot_general(block, panel, (((1,), (1,)), ((), ())), preferred_element_type=F32)


def times(block, panel):
    return lax.dot_general(block, panel, (((1,), (0,)), ((), ())), preferred_element_type=F32)


def operator_blocks(me_ref, profile_ref, table_ref, a_ref, out_ref, step_ref):
    rows, full = a_ref.shape
    pad = out_ref.shape[1]
    step_ref[...] = jnp.full(step_ref.shape, table_ref[profile_ref[0]], F32)
    for block in range(full // rows):
        place = me_ref[0] ^ block
        out_ref[place, rows // 16 * 16 :, :] = jnp.zeros((pad - rows // 16 * 16, pad), BF16)
        out_ref[place, :, rows // LANES * LANES :] = jnp.zeros((pad, pad - rows // LANES * LANES), BF16)
        out_ref[place, :rows, :rows] = a_ref[:, block * rows : (block + 1) * rows]


def turned(me_ref, x_ref, *refs):
    tall = refs[-1]
    rows = x_ref.shape[0]
    tall[rows:, :] = jnp.zeros_like(tall[rows:, :])
    tall[:rows, :] = x_ref[...].astype(F32)
    flat = tall[...].T.astype(BF16)
    first = 0
    for out_ref in refs[:-1]:
        out_ref[...] = flat[first : first + out_ref.shape[0]]
        first += out_ref.shape[0]


def coupling(reflect_ref, cotangent_ref, out_ref, tall):
    levels, rows, _, columns = reflect_ref.shape
    pad = tall.shape[0]
    group, part = out_ref.shape[:2]
    tall[rows:, :] = jnp.zeros_like(tall[rows:, :])
    cot = cotangent_ref[...].T
    high = cot.astype(BF16)
    low = (cot - high.astype(F32)).astype(BF16)
    tracked = cot.shape[1]
    first = levels * pad
    out_ref[:, :, first : first + tracked] = high.reshape(group, part, tracked)
    out_ref[:, :, first + tracked :] = low.reshape(group, part, tracked)
    for level in range(levels):
        tall[:rows, :] = reflect_ref[level, :, 0, :]
        out_ref[:, :, level * pad : (level + 1) * pad] = tall[...].T.astype(BF16).reshape(group, part, pad)


def halved(value_ref, *refs):
    split(refs, value_ref[...])


def forward_most(own_ref, core_ref, far_ref, panel_ref, out_ref):
    near = times_t(own_ref[...], panel_ref[0]) + times_t(core_ref[...], panel_ref[1])
    out_ref[...] = near + times_t(far_ref[...], panel_ref[2])


def forward_last(degree, step_ref, x_ref, most_ref, panel_ref, *refs):
    product = most_ref[...] + times_t(joined(refs[:HALVES]), panel_ref[3])
    value = (x_ref[...].astype(F32) + step_ref[0:1, 0:1] / degree * product).astype(BF16)
    out_ref = refs[-1]
    first = 0
    for ref in refs[HALVES:-1]:
        out_ref[first : first + ref.shape[0]] = ref[...]
        first += ref.shape[0]
    out_ref[first:] = value


def merge(levels, rows, me_ref, order_ref, w_ref, rc_ref, field_ref, cmap_ref, level_ref, sums_ref):
    group, part, pad = w_ref.shape
    tracked = order_ref.shape[1]
    tail = level_ref.shape[2]
    place = lax.broadcasted_iota(jnp.int32, (pad, tracked), 0)
    order = place + lax.rem(me_ref[0] * rows, ORDERS)
    for _ in range(-(-rows // ORDERS)):
        order = jnp.where(order >= ORDERS, order - ORDERS, order)
    order = jnp.where(place < rows, order, -1)
    onehot = jnp.where(order == order_ref[...], 1.0, 0.0).astype(BF16)
    onehot = jnp.concatenate([onehot, onehot], axis=1)
    totals = []
    merged = [w_ref[s].astype(F32) for s in range(group)]
    level_ref[...] = rc_ref[:, :, :tail]
    for level in range(levels):
        sent = [
            rc_ref[s, :, level * pad : (level + 1) * pad].astype(F32) * merged[s] for s in range(group)
        ]
        merged = [merged[s] + sent[s ^ 2**level] for s in range(group)]
    lane = lax.broadcasted_iota(jnp.int32, (part, LANES), 1)
    cmaps = times_t(rc_ref[:, :, tail:].reshape(group * part, 2 * tracked), onehot).reshape(group, part, pad)
    for s in range(group):
        field = merged[s]
        cmap = cmaps[s]
        squared = field * field
        power = jnp.sum(squared, axis=1, keepdims=True)
        weighted = jnp.sum(cmap * squared, axis=1, keepdims=True)
        field_ref[s] = field
        cmap_ref[s] = cmap
        totals.append(jnp.where(lane == 0, power, jnp.where(lane == 1, weighted, 0.0)))
    sums_ref[...] = jnp.concatenate(totals, axis=0).T[: sums_ref.shape[0]]


def unmerge(levels, full, scale, field_ref, cmap_ref, rc_ref, s0, s1, s2, s3, out_ref):
    group, part, pad = field_ref.shape
    sums = (s0[...] + s1[...]) + (s2[...] + s3[...])
    sums = jnp.concatenate([sums] * (LANES // sums.shape[0]), axis=0).T
    grad = []
    for s in range(group):
        power = sums[s * part : (s + 1) * part, 0:1]
        weighted = sums[s * part : (s + 1) * part, 1:2]
        inverse = 1.0 / (power / full + 1e-06)
        first = scale * 2.0 * inverse
        second = scale * 2.0 / full * (weighted * inverse * inverse)
        grad.append((first * cmap_ref[s] - second) * field_ref[s])
    for level in range(levels - 1, -1, -1):
        grad = [
            grad[s]
            + rc_ref[s, :, level * pad : (level + 1) * pad].astype(F32) * grad[s ^ 2**level]
            for s in range(group)
        ]
    for s in range(group):
        out_ref[s] = grad[s].astype(BF16)


def columns_of(me_ref, *refs):
    out_ref, pile = refs[-2:]
    places = pile.shape[0]
    rows = out_ref.shape[1] // places
    first = 0
    each = places - 1 + HALVES
    for chunk in range((len(refs) - 2) // each):
        group = refs[chunk * each : (chunk + 1) * each]
        width = group[0].shape[0]
        for place in range(places - 1):
            pile[me_ref[0] ^ place, first : first + width, :] = group[place][...]
        pile[me_ref[0] ^ (places - 1), first : first + width, :] = joined(group[places - 1 :])
        first += width
    for block in range(places):
        out_ref[:, block * rows : (block + 1) * rows] = pile[block, :, :rows]


def backward_first(first, step_ref, whole_ref, panel_ref, scaled_ref, total_ref, *refs):
    width = scaled_ref.shape[0]
    upstream = whole_ref[first : first + width]
    for ref in refs[HALVES:]:
        ref[...] = whole_ref[width:]
    total_ref[...] = upstream.astype(F32)
    scaled = (step_ref[0:1, 0:1] * upstream.astype(F32)).astype(BF16)
    scaled_ref[...] = scaled
    split(refs[:HALVES], times(scaled, panel_ref[3]).astype(BF16))


def backward_next(degree, step_ref, near_ref, core_ref, far_ref, before_ref, panel_ref, scaled_ref, total_ref, *sent):
    upstream = near_ref[...] + core_ref[...].astype(F32) + far_ref[...].astype(F32)
    total_ref[...] = before_ref[...] + upstream
    scaled = (step_ref[0:1, 0:1] / degree * upstream).astype(BF16)
    scaled_ref[...] = scaled
    split(sent, times(scaled, panel_ref[3]).astype(BF16))


def backward_most(scaled_ref, panel_ref, sent_ref, near_ref, most_ref):
    scaled = scaled_ref[...]
    most_ref[...] = times(scaled, panel_ref[2])
    sent_ref[...] = times(scaled, panel_ref[1]).astype(BF16)
    near_ref[...] = times(scaled, panel_ref[0])


def backward_last(most_ref, *refs):
    refs[-1][...] = (most_ref[...] + joined(refs[:-1]).astype(F32)).astype(BF16)


def outer(chunks, *refs):
    out_ref = refs[-1]
    rights = refs[TAYLOR * chunks : TAYLOR * chunks + TAYLOR]
    total = None
    for degree, right in enumerate(rights):
        left = jnp.concatenate([ref[...] for ref in refs[degree * chunks : (degree + 1) * chunks]], axis=0)
        value = lax.dot_general(left, right[...], (((0,), (0,)), ((), ())), preferred_element_type=F32)
        total = value if total is None else total + value
    out_ref[:, 0, :] = total


def outer_rows(first, tiles, lefts, rights, target, rows, full):
    body = functools.partial(outer, len(lefts) // TAYLOR)
    specs = [pl.BlockSpec((left.shape[0], LANES), lambda i: (0, i + first)) for left in lefts]
    args = [*lefts, *rights[::-1]]
    if target is not None:
        args.append(target)
    return pl.pallas_call(
        body,
        grid=(tiles,),
        out_shape=shape(rows, 1, full),
        in_specs=specs + [WHOLE] * TAYLOR + [pl.BlockSpec(memory_space=pl.ANY)] * (target is not None),
        out_specs=pl.BlockSpec((LANES, 1, full), lambda i: (i + first, 0, 0)),
        input_output_aliases={} if target is None else {len(args) - 1: 0},
        compiler_params=pltpu.CompilerParams(vmem_limit_bytes=20 * 2**20),
        cost_estimate=pl.CostEstimate(flops=0 if target is None else COST, transcendentals=0, bytes_accessed=1),
    )(*args)


def finish(*refs):
    out_ref = refs[-1]
    rows = out_ref.shape[0]
    values = []
    for chunk in range(len(refs) // 4):
        near, total, core, far = (ref[...].astype(F32) for ref in refs[4 * chunk : 4 * chunk + 4])
        values.append((near + total) + (core + far))
    value = jnp.concatenate(values, axis=0).T
    out_ref[:, 0, :] = value[:rows]


def local(operator, incident, reflect, thickness_table, profile, order_index, cotangent):
    rows, full = operator.shape[1:]
    columns = incident.shape[2]
    levels = reflect.shape[1]
    group = 2**levels
    tracked = order_index.shape[0]
    pad = -(-rows // LANES) * LANES
    part = columns // group
    count = range(CHUNKS)
    me = lax.axis_index("row")
    me_arr = me.reshape(1)
    widths = [columns * share // sum(SPLIT) for share in SPLIT]
    blocks = [shape(width, pad, dtype=BF16) for width in widths]
    wides = [shape(width, pad) for width in widths]
    parts = [[shape(width // HALVES, pad, dtype=BF16)] * HALVES for width in widths]

    rc = call(
        coupling,
        shape(group, part, levels * pad + 2 * tracked, dtype=BF16),
        reflect.transpose(1, 2, 0, 3),
        cotangent[0],
        scratch=[pltpu.VMEM((pad, columns), F32)],
        limit=10,
    )
    x = call(turned, blocks, after(me_arr, rc), incident[0], scratch=[pltpu.VMEM((pad, columns), F32)])
    rc = over_cuts(rc)
    fars = [over_row(value, 2) for value in x]
    cores = [over_row(value, 1) for value in x]
    panel, step = call(
        operator_blocks,
        (shape(4, pad, pad, dtype=BF16), shape(8, LANES)),
        after(me_arr, x[0]), profile, thickness_table, operator[0],
        limit=12,
    )
    token = panel

    current = list(x)
    stored = [[] for _ in count]
    rights = []
    x = list(x)

    def write_columns(place, pieces, hbm=True):
        return call(
            columns_of,
            (pltpu.HBM if hbm else jax.ShapeDtypeStruct)((columns, full), BF16),
            place, *pieces,
            scratch=[pltpu.VMEM((4, columns, pad), BF16)],
            limit=6,
        )

    for degree in range(TAYLOR, 0, -1):
        next_fars, next_cores = [], []
        for chunk in count:
            far = after(fars[chunk], token)
            halves = call(halved, parts[chunk], far)
            most = call(
                forward_most, wides[chunk], current[chunk], after(cores[chunk], halves[0]), far, panel
            )
            diag = [over_row(half, 1) for half in halves]
            stored[chunk].append((current[chunk], cores[chunk], far, *diag))
            final = degree == 1 and chunk == CHUNKS - 1
            value = call(
                functools.partial(forward_last, degree),
                pltpu.HBM((columns, pad), BF16) if final else blocks[chunk],
                step, x[chunk], most, panel, *diag,
                *(current[:-1] if final else []),
            )
            current[chunk] = value
            token = value
            if degree > 1:
                next_fars.append(over_row(value, 2))
                next_cores.append(over_row(value, 1))
        fars, cores = next_fars, next_cores
        pieces = [piece for chunk in count for piece in stored[chunk][-1]]
        place = after(me_arr, token)
        token = write_columns(place, pieces)
        rights.append(token)

    current[-1], rc, token = lax.optimization_barrier((current[-1], rc, token))
    rights[-1] = token
    swapped = over_cuts(current[-1].reshape(group, part, pad))
    field, cmap, coupled, sums = call(
        functools.partial(merge, levels, rows),
        (
            shape(group, part, pad),
            shape(group, part, pad),
            shape(group, part, levels * pad, dtype=BF16),
            shape(8, group * part),
        ),
        me_arr, order_index.reshape(1, tracked), swapped, rc,
        limit=12,
    )
    s1, s2, s3 = (over_row(sums, mask) for mask in (1, 2, 3))
    grad = call(
        functools.partial(unmerge, levels, full, 1.0 / math.sqrt(columns)),
        pltpu.HBM((group, part, pad), BF16),
        field, cmap, coupled, sums, s1, s2, s3,
    )
    whole = over_cuts(grad).reshape(columns, pad)
    token = whole

    total = [None] * CHUNKS
    pending = [None] * CHUNKS
    scaled_all = []
    for degree in range(1, TAYLOR + 1):
        for chunk in count:
            outs = [blocks[chunk], wides[chunk]] + parts[chunk]
            if degree == 1:
                scaled, total[chunk], *sent = call(
                    functools.partial(backward_first, 0),
                    outs + ([blocks[1]] if chunk == 0 and CHUNKS == 2 else []),
                    step, after(whole, token), panel,
                )
                if chunk == 0 and CHUNKS == 2:
                    whole = sent.pop()
            else:
                near, core, far = pending[chunk]
                scaled, total[chunk], *sent = call(
                    functools.partial(backward_next, degree), outs,
                    step, near, core, after(far, token), total[chunk], panel,
                )
            scaled_all.append(scaled)
            diag = [over_row(half, 1) for half in sent]
            sent, near, most = call(
                backward_most, [blocks[chunk], wides[chunk], wides[chunk]], after(scaled, sent[0]), panel
            )
            core = over_row(sent, 1)
            sent = call(backward_last, blocks[chunk], most, *diag)
            far = over_row(sent, 2)
            token = sent
            pending[chunk] = (near, core, far)
    lefts = [*scaled_all[:-1], after(scaled_all[-1], token)]
    tiles = -(-rows // LANES)
    top = tiles * 3 // 5
    grad_matrix = outer_rows(0, top, lefts, rights, None, rows, full)
    for late in pending[:-1]:
        grad_matrix = after(grad_matrix, late[2])
    grad_matrix = outer_rows(top, tiles - top, lefts, rights, grad_matrix, rows, full)
    args = []
    for chunk in count:
        near, core, far = pending[chunk]
        args += [near, total[chunk], core, far]
    args[-1] = after(args[-1], grad_matrix)
    grad_incident = call(finish, shape(rows, 1, columns), *args)
    return (grad_matrix.transpose(1, 0, 2), grad_incident.transpose(1, 0, 2))


def solution(mesh):
    return jax.shard_map(
        local,
        mesh=mesh,
        in_specs=(
            P("cuts", "row", None),
            P("cuts", "row", None),
            P("cuts", None, "row", None),
            P(),
            P("cuts"),
            P(),
            P("cuts", None, None),
        ),
        out_specs=(P("cuts", "row", None), P("cuts", "row", None)),
        check_vma=False,
    )
```

```python
import functools
import math

import jax
import jax.numpy as jnp
from jax import lax
from jax.experimental import pallas as pl
from jax.experimental.pallas import tpu as pltpu
from jax.sharding import PartitionSpec as P

ORDERS = 601
TAYLOR = 3
LEVELS = 3
SPLIT = (128, 128)
CHUNKS = len(SPLIT)
LANES = 128
COST = 5000000000
HALVES = 2
F32 = jnp.float32
BF16 = jnp.bfloat16
WHOLE = pl.BlockSpec(memory_space=pltpu.VMEM)
SCALAR = pl.BlockSpec(memory_space=pltpu.SMEM)


def shape(*dims, dtype=F32):
    return jax.ShapeDtypeStruct(dims, dtype)


def call(body, out_shape, *args, scratch=(), limit=8):
    return pl.pallas_call(
        body,
        out_shape=out_shape,
        in_specs=[SCALAR if arg.size <= 8 else WHOLE for arg in args],
        out_specs=jax.tree.map(lambda _: WHOLE, out_shape),
        scratch_shapes=list(scratch),
        compiler_params=pltpu.CompilerParams(vmem_limit_bytes=limit * 2**20),
        cost_estimate=pl.CostEstimate(flops=0, transcendentals=0, bytes_accessed=1),
    )(*args)


def split(refs, value):
    first = 0
    for ref in refs:
        ref[...] = value[first : first + ref.shape[0]]
        first += ref.shape[0]


def joined(refs):
    return jnp.concatenate([ref[...] for ref in refs], axis=0)


def after(value, token):
    return lax.optimization_barrier((value, token))[0]


def over_row(value, mask):
    pairs = [(source, source ^ mask) for source in range(lax.axis_size("row"))]
    return lax.ppermute(value, "row", pairs)


def over_cuts(value):
    size = lax.axis_size("cuts")
    group = 2**LEVELS
    groups = None
    if size != group:
        groups = [list(range(first, first + group)) for first in range(0, size, group)]
    return lax.all_to_all(value, "cuts", 0, 0, axis_index_groups=groups, tiled=True)


def times_t(block, panel):
    return lax.dot_general(block, panel, (((1,), (1,)), ((), ())), preferred_element_type=F32)


def times(block, panel):
    return lax.dot_general(block, panel, (((1,), (0,)), ((), ())), preferred_element_type=F32)


def operator_blocks(me_ref, profile_ref, table_ref, a_ref, out_ref, step_ref):
    rows, full = a_ref.shape
    pad = out_ref.shape[1]
    step_ref[...] = jnp.full(step_ref.shape, table_ref[profile_ref[0]], F32)
    for block in range(full // rows):
        place = me_ref[0] ^ block
        out_ref[place, rows // 16 * 16 :, :] = jnp.zeros((pad - rows // 16 * 16, pad), BF16)
        out_ref[place, :, rows // LANES * LANES :] = jnp.zeros((pad, pad - rows // LANES * LANES), BF16)
        out_ref[place, :rows, :rows] = a_ref[:, block * rows : (block + 1) * rows]


def turned(me_ref, x_ref, *refs):
    tall = refs[-1]
    rows = x_ref.shape[0]
    tall[rows:, :] = jnp.zeros_like(tall[rows:, :])
    tall[:rows, :] = x_ref[...].astype(F32)
    flat = tall[...].T.astype(BF16)
    first = 0
    for out_ref in refs[:-1]:
        out_ref[...] = flat[first : first + out_ref.shape[0]]
        first += out_ref.shape[0]


def coupling(levels, reflect_ref, cotangent_ref, out_ref, tall):
    rows = reflect_ref.shape[1]
    pad = tall.shape[0]
    group, part = out_ref.shape[:2]
    level = pl.program_id(0)

    @pl.when(level < levels)
    def _():
        tall[rows // 8 * 8 :, :] = jnp.zeros_like(tall[rows // 8 * 8 :, :])
        tall[:rows, :] = reflect_ref[0, :, 0, :]
        out_ref[...] = tall[...].T.astype(BF16).reshape(group, part, pad)

    @pl.when(level == levels)
    def _():
        cot = cotangent_ref[...].T
        high = cot.astype(BF16)
        low = (cot - high.astype(F32)).astype(BF16)
        tracked = cot.shape[1]
        out_ref[:, :, :tracked] = high.reshape(group, part, tracked)
        out_ref[:, :, tracked : 2 * tracked] = low.reshape(group, part, tracked)


def halved(value_ref, *refs):
    split(refs, value_ref[...])


def forward_most(own_ref, core_ref, far_ref, panel_ref, out_ref):
    near = times_t(own_ref[...], panel_ref[0]) + times_t(core_ref[...], panel_ref[1])
    out_ref[...] = near + times_t(far_ref[...], panel_ref[2])


def forward_last(degree, step_ref, x_ref, most_ref, panel_ref, *refs):
    product = most_ref[...] + times_t(joined(refs[:-1]), panel_ref[3])
    refs[-1][...] = (x_ref[...].astype(F32) + step_ref[0:1, 0:1] / degree * product).astype(BF16)


def forward_end(step_ref, x_ref, most_ref, panel_ref, me_ref, before_ref, *refs):
    out_ref, pile_ref = refs[-2:]
    pieces = refs[:-2]
    diag = pieces[-HALVES:]
    product = most_ref[...] + times_t(joined(diag), panel_ref[3])
    value = (x_ref[...].astype(F32) + step_ref[0:1, 0:1] * product).astype(BF16)
    first = before_ref.shape[0]
    out_ref[:first] = before_ref[...]
    out_ref[first:] = value
    places = pile_ref.shape[0]
    each = places - 1 + HALVES
    row = 0
    for chunk in range(len(pieces) // each):
        group = pieces[chunk * each : (chunk + 1) * each]
        width = group[0].shape[0]
        for place in range(places - 1):
            pile_ref[me_ref[0] ^ place, row : row + width, :] = group[place][...]
        pile_ref[me_ref[0] ^ (places - 1), row : row + width, :] = joined(group[places - 1 :])
        row += width


def columns_from(pile_ref, out_ref):
    places = pile_ref.shape[0]
    rows = out_ref.shape[1] // places
    for block in range(places):
        out_ref[:, block * rows : (block + 1) * rows] = pile_ref[block, :, :rows]


def merge(levels, rows, me_ref, order_ref, w_ref, rc_ref, field_ref, cmap_ref, level_ref, sums_ref):
    group, part, pad = w_ref.shape
    tracked = order_ref.shape[1]
    tail = level_ref.shape[2]
    place = lax.broadcasted_iota(jnp.int32, (pad, tracked), 0)
    order = place + lax.rem(me_ref[0] * rows, ORDERS)
    for _ in range(-(-rows // ORDERS)):
        order = jnp.where(order >= ORDERS, order - ORDERS, order)
    order = jnp.where(place < rows, order, -1)
    onehot = jnp.where(order == order_ref[...], 1.0, 0.0).astype(BF16)
    onehot = jnp.concatenate([onehot, onehot], axis=1)
    totals = []
    merged = [w_ref[s].astype(F32) for s in range(group)]
    level_ref[...] = rc_ref[:, :, :tail]
    for level in range(levels):
        sent = [
            rc_ref[s, :, level * pad : (level + 1) * pad].astype(F32) * merged[s] for s in range(group)
        ]
        merged = [merged[s] + sent[s ^ 2**level] for s in range(group)]
    lane = lax.broadcasted_iota(jnp.int32, (part, LANES), 1)
    cmaps = times_t(rc_ref[:, :, tail:].reshape(group * part, 2 * tracked), onehot).reshape(group, part, pad)
    for s in range(group):
        field = merged[s]
        cmap = cmaps[s]
        squared = field * field
        power = jnp.sum(squared, axis=1, keepdims=True)
        weighted = jnp.sum(cmap * squared, axis=1, keepdims=True)
        field_ref[s] = field
        cmap_ref[s] = cmap
        totals.append(jnp.where(lane == 0, power, jnp.where(lane == 1, weighted, 0.0)))
    sums_ref[...] = jnp.concatenate(totals, axis=0).T[: sums_ref.shape[0]]


def unmerge(levels, full, scale, field_ref, cmap_ref, rc_ref, s0, s1, s2, s3, out_ref):
    group, part, pad = field_ref.shape
    sums = (s0[...] + s1[...]) + (s2[...] + s3[...])
    sums = jnp.concatenate([sums] * (LANES // sums.shape[0]), axis=0).T
    grad = []
    for s in range(group):
        power = sums[s * part : (s + 1) * part, 0:1]
        weighted = sums[s * part : (s + 1) * part, 1:2]
        inverse = 1.0 / (power / full + 1e-06)
        first = scale * 2.0 * inverse
        second = scale * 2.0 / full * (weighted * inverse * inverse)
        grad.append((first * cmap_ref[s] - second) * field_ref[s])
    for level in range(levels - 1, -1, -1):
        grad = [
            grad[s]
            + rc_ref[s, :, level * pad : (level + 1) * pad].astype(F32) * grad[s ^ 2**level]
            for s in range(group)
        ]
    for s in range(group):
        out_ref[s] = grad[s].astype(BF16)


def columns_of(me_ref, *refs):
    out_ref, pile = refs[-2:]
    places = pile.shape[0]
    rows = out_ref.shape[1] // places
    first = 0
    each = places - 1 + HALVES
    for chunk in range((len(refs) - 2) // each):
        group = refs[chunk * each : (chunk + 1) * each]
        width = group[0].shape[0]
        for place in range(places - 1):
            pile[me_ref[0] ^ place, first : first + width, :] = group[place][...]
        pile[me_ref[0] ^ (places - 1), first : first + width, :] = joined(group[places - 1 :])
        first += width
    for block in range(places):
        out_ref[:, block * rows : (block + 1) * rows] = pile[block, :, :rows]


def backward_first(first, step_ref, whole_ref, panel_ref, scaled_ref, total_ref, *refs):
    width = scaled_ref.shape[0]
    upstream = whole_ref[first : first + width]
    for ref in refs[HALVES:]:
        ref[...] = whole_ref[width:]
    total_ref[...] = upstream.astype(F32)
    scaled = (step_ref[0:1, 0:1] * upstream.astype(F32)).astype(BF16)
    scaled_ref[...] = scaled
    split(refs[:HALVES], times(scaled, panel_ref[3]).astype(BF16))


def backward_next(degree, step_ref, near_ref, core_ref, far_ref, before_ref, panel_ref, scaled_ref, total_ref, *sent):
    upstream = near_ref[...] + core_ref[...].astype(F32) + far_ref[...].astype(F32)
    total_ref[...] = before_ref[...] + upstream
    scaled = (step_ref[0:1, 0:1] / degree * upstream).astype(BF16)
    scaled_ref[...] = scaled
    split(sent, times(scaled, panel_ref[3]).astype(BF16))


def backward_most(scaled_ref, panel_ref, sent_ref, near_ref, most_ref):
    scaled = scaled_ref[...]
    most_ref[...] = times(scaled, panel_ref[2])
    sent_ref[...] = times(scaled, panel_ref[1]).astype(BF16)
    near_ref[...] = times(scaled, panel_ref[0])


def backward_last(most_ref, *refs):
    refs[-1][...] = (most_ref[...] + joined(refs[:-1]).astype(F32)).astype(BF16)


def product_rows(lefts, right, columns):
    left = jnp.concatenate([ref[:, columns] for ref in lefts], axis=0)
    return lax.dot_general(left, right[...], (((0,), (0,)), ((), ())), preferred_element_type=F32)


def outer_early(*refs):
    rights, out_ref = refs[-TAYLOR:-1], refs[-1]
    chunks = (len(refs) - TAYLOR) // len(rights)

    @pl.loop(0, out_ref.shape[0] // LANES)
    def _(tile):
        place = pl.ds(pl.multiple_of(tile * LANES, LANES), LANES)
        values = [
            product_rows(refs[term * chunks : (term + 1) * chunks], right, place)
            for term, right in enumerate(rights)
        ]
        out_ref[place, :] = functools.reduce(jnp.add, values)


def outer(chunks, first, *refs):
    right, early, out_ref = refs[chunks], refs[chunks + 1], refs[-1]
    tile = pl.program_id(0) + first
    place = pl.ds(pl.multiple_of(tile * LANES, LANES), LANES)
    out_ref[:, 0, :] = product_rows(refs[:chunks], right, slice(None)) + early[place, :]


def outer_rows(first, tiles, lefts, right, early, target, rows, full):
    specs = [pl.BlockSpec((left.shape[0], LANES), lambda i: (0, i + first)) for left in lefts]
    args = [*lefts, right, early]
    if target is not None:
        args.append(target)
    return pl.pallas_call(
        functools.partial(outer, len(lefts), first),
        grid=(tiles,),
        out_shape=shape(rows, 1, full),
        in_specs=specs + [WHOLE] * 2 + [pl.BlockSpec(memory_space=pl.ANY)] * (target is not None),
        out_specs=pl.BlockSpec((LANES, 1, full), lambda i: (i + first, 0, 0)),
        input_output_aliases={} if target is None else {len(args) - 1: 0},
        compiler_params=pltpu.CompilerParams(vmem_limit_bytes=16 * 2**20),
        cost_estimate=pl.CostEstimate(flops=0 if target is None else COST, transcendentals=0, bytes_accessed=1),
    )(*args)


def finish(*refs):
    out_ref = refs[-1]
    rows = out_ref.shape[0]
    values = []
    for chunk in range(len(refs) // 4):
        near, total, core, far = (ref[...].astype(F32) for ref in refs[4 * chunk : 4 * chunk + 4])
        values.append((near + total) + (core + far))
    value = jnp.concatenate(values, axis=0).T
    out_ref[:, 0, :] = value[:rows]


def local(operator, incident, reflect, thickness_table, profile, order_index, cotangent):
    rows, full = operator.shape[1:]
    columns = incident.shape[2]
    levels = reflect.shape[1]
    group = 2**levels
    tracked = order_index.shape[0]
    pad = -(-rows // LANES) * LANES
    part = columns // group
    count = range(CHUNKS)
    me = lax.axis_index("row")
    me_arr = me.reshape(1)
    widths = [columns * share // sum(SPLIT) for share in SPLIT]
    blocks = [shape(width, pad, dtype=BF16) for width in widths]
    wides = [shape(width, pad) for width in widths]
    parts = [[shape(width // HALVES, pad, dtype=BF16)] * HALVES for width in widths]

    rc = pl.pallas_call(
        functools.partial(coupling, levels),
        grid=(levels + 1,),
        out_shape=pltpu.HBM((group, part, levels * pad + 2 * tracked), BF16),
        in_specs=[
            pl.BlockSpec((1, rows, 1, columns), lambda i: (jnp.minimum(i, levels - 1), 0, 0, 0)),
            pl.BlockSpec((tracked, columns), lambda i: (0, 0)),
        ],
        out_specs=pl.BlockSpec((group, part, pad), lambda i: (0, 0, i)),
        scratch_shapes=[pltpu.VMEM((pad, columns), F32)],
        compiler_params=pltpu.CompilerParams(vmem_limit_bytes=10 * 2**20),
        cost_estimate=pl.CostEstimate(flops=0, transcendentals=0, bytes_accessed=1),
    )(
        pltpu.with_memory_space_constraint(reflect.transpose(1, 2, 0, 3), pltpu.HBM),
        pltpu.with_memory_space_constraint(cotangent[0], pltpu.HBM),
    )
    x = call(turned, blocks, after(me_arr, rc), incident[0], scratch=[pltpu.VMEM((pad, columns), F32)])
    rc = over_cuts(rc)
    fars = [over_row(value, 2) for value in x]
    cores = [over_row(value, 1) for value in x]
    panel, step = call(
        operator_blocks,
        (shape(4, pad, pad, dtype=BF16), shape(8, LANES)),
        after(me_arr, x[0]), profile, thickness_table, operator[0],
        limit=12,
    )
    token = panel

    current = list(x)
    stored = [[] for _ in count]
    rights = []
    x = list(x)

    def write_columns(place, pieces, hbm=True):
        return call(
            columns_of,
            (pltpu.HBM if hbm else jax.ShapeDtypeStruct)((columns, full), BF16),
            place, *pieces,
            scratch=[pltpu.VMEM((4, columns, pad), BF16)],
            limit=6,
        )

    for degree in range(TAYLOR, 0, -1):
        next_fars, next_cores = [], []
        for chunk in count:
            far = after(fars[chunk], token)
            halves = call(halved, parts[chunk], far)
            most = call(
                forward_most, wides[chunk], current[chunk], after(cores[chunk], halves[0]), far, panel
            )
            diag = [over_row(half, 1) for half in halves]
            stored[chunk].append((current[chunk], cores[chunk], far, *diag))
            if degree == 1 and chunk == CHUNKS - 1:
                value, pile = call(
                    forward_end,
                    (pltpu.HBM((columns, pad), BF16), pltpu.HBM((4, columns, pad), BF16)),
                    step, x[chunk], most, panel, me_arr, current[0],
                    *[piece for each in count for piece in stored[each][-1]],
                )
            else:
                value = call(
                    functools.partial(forward_last, degree),
                    blocks[chunk], step, x[chunk], most, panel, *diag,
                )
            current[chunk] = value
            token = value
            if degree > 1:
                next_fars.append(over_row(value, 2))
                next_cores.append(over_row(value, 1))
        fars, cores = next_fars, next_cores
        pieces = [piece for chunk in count for piece in stored[chunk][-1]]
        place = after(me_arr, token)
        if degree > 1:
            token = write_columns(place, pieces)
            rights.append(token)

    current[-1], rc = lax.optimization_barrier((current[-1], rc))
    swapped = over_cuts(current[-1].reshape(group, part, pad))
    field, cmap, coupled, sums = call(
        functools.partial(merge, levels, rows),
        (
            shape(group, part, pad),
            shape(group, part, pad),
            shape(group, part, levels * pad, dtype=BF16),
            shape(8, group * part),
        ),
        me_arr, order_index.reshape(1, tracked), swapped, rc,
        limit=12,
    )
    s1, s2, s3 = (over_row(sums, mask) for mask in (1, 2, 3))
    grad = call(
        functools.partial(unmerge, levels, full, 1.0 / math.sqrt(columns)),
        pltpu.HBM((group, part, pad), BF16),
        field, cmap, coupled, sums, s1, s2, s3,
    )
    whole = over_cuts(grad).reshape(columns, pad)
    token = whole

    total = [None] * CHUNKS
    pending = [None] * CHUNKS
    scaled_all = []
    for degree in range(1, TAYLOR + 1):
        for chunk in count:
            outs = [blocks[chunk], wides[chunk]] + parts[chunk]
            if degree == 1:
                scaled, total[chunk], *sent = call(
                    functools.partial(backward_first, 0),
                    outs + ([blocks[1]] if chunk == 0 and CHUNKS == 2 else []),
                    step, after(whole, token), panel,
                )
                if chunk == 0 and CHUNKS == 2:
                    whole = sent.pop()
            else:
                near, core, far = pending[chunk]
                scaled, total[chunk], *sent = call(
                    functools.partial(backward_next, degree), outs,
                    step, near, core, after(far, token), total[chunk], panel,
                )
            scaled_all.append(scaled)
            diag = [over_row(half, 1) for half in sent]
            sent, near, most = call(
                backward_most, [blocks[chunk], wides[chunk], wides[chunk]], after(scaled, sent[0]), panel
            )
            core = over_row(sent, 1)
            sent = call(backward_last, blocks[chunk], most, *diag)
            far = over_row(sent, 2)
            token = sent
            pending[chunk] = (near, core, far)
            if degree == 1 and chunk == CHUNKS - 1:
                token = call(columns_from, shape(columns, full, dtype=BF16), after(pile, token))
                rights.append(token)
            if degree == TAYLOR - 1 and chunk == CHUNKS - 1:
                early = call(
                    outer_early,
                    shape(pad, full),
                    *scaled_all[:-1], after(scaled_all[-1], token), *rights[:0:-1],
                    limit=12,
                )
                token = early
    lefts = [*scaled_all[-CHUNKS:-1], after(scaled_all[-1], token)]
    tiles = -(-rows // LANES)
    top = tiles * 3 // 5
    grad_matrix = outer_rows(0, top, lefts, rights[0], early, None, rows, full)
    for late in pending[:-1]:
        grad_matrix = after(grad_matrix, late[2])
    grad_matrix = outer_rows(top, tiles - top, lefts, rights[0], early, grad_matrix, rows, full)
    args = []
    for chunk in count:
        near, core, far = pending[chunk]
        args += [near, total[chunk], core, far]
    args[-1] = after(args[-1], grad_matrix)
    grad_incident = call(finish, shape(rows, 1, columns), *args)
    return (grad_matrix.transpose(1, 0, 2), grad_incident.transpose(1, 0, 2))


def solution(mesh):
    return jax.shard_map(
        local,
        mesh=mesh,
        in_specs=(
            P("cuts", "row", None),
            P("cuts", "row", None),
            P("cuts", None, "row", None),
            P(),
            P("cuts"),
            P(),
            P("cuts", None, None),
        ),
        out_specs=(P("cuts", "row", None), P("cuts", "row", None)),
        check_vma=False,
    )
```

```python
import functools
import math

import jax
import jax.numpy as jnp
from jax import lax
from jax.experimental import pallas as pl
from jax.experimental.pallas import tpu as pltpu
from jax.sharding import PartitionSpec as P

ORDERS = 601
TAYLOR = 3
LEVELS = 3
SPLIT = (128, 128)
CHUNKS = len(SPLIT)
LANES = 128
COST = 5000000000
HALVES = 2
F32 = jnp.float32
BF16 = jnp.bfloat16
WHOLE = pl.BlockSpec(memory_space=pltpu.VMEM)
SCALAR = pl.BlockSpec(memory_space=pltpu.SMEM)
ANY = pl.BlockSpec(memory_space=pl.ANY)


def shape(*dims, dtype=F32):
    return jax.ShapeDtypeStruct(dims, dtype)


def call(body, out_shape, *args, scratch=(), limit=8):
    return pl.pallas_call(
        body,
        out_shape=out_shape,
        in_specs=[SCALAR if arg.size <= 8 else WHOLE for arg in args],
        out_specs=jax.tree.map(lambda _: WHOLE, out_shape),
        scratch_shapes=list(scratch),
        compiler_params=pltpu.CompilerParams(vmem_limit_bytes=limit * 2**20),
        cost_estimate=pl.CostEstimate(flops=0, transcendentals=0, bytes_accessed=1),
    )(*args)


def split(refs, value):
    first = 0
    for ref in refs:
        ref[...] = value[first : first + ref.shape[0]]
        first += ref.shape[0]


def joined(refs):
    return jnp.concatenate([ref[...] for ref in refs], axis=0)


def after(value, token):
    return lax.optimization_barrier((value, token))[0]


def over_row(value, mask):
    pairs = [(source, source ^ mask) for source in range(lax.axis_size("row"))]
    return lax.ppermute(value, "row", pairs)


def over_cuts(value):
    size = lax.axis_size("cuts")
    group = 2**LEVELS
    groups = None
    if size != group:
        groups = [list(range(first, first + group)) for first in range(0, size, group)]
    return lax.all_to_all(value, "cuts", 0, 0, axis_index_groups=groups, tiled=True)


def times_t(block, panel):
    return lax.dot_general(block, panel, (((1,), (1,)), ((), ())), preferred_element_type=F32)


def times(block, panel):
    return lax.dot_general(block, panel, (((1,), (0,)), ((), ())), preferred_element_type=F32)


def operator_blocks(me_ref, profile_ref, table_ref, a_ref, out_ref, step_ref):
    rows, full = a_ref.shape
    pad = out_ref.shape[1]
    step_ref[...] = jnp.full(step_ref.shape, table_ref[profile_ref[0]], F32)
    for block in range(full // rows):
        place = me_ref[0] ^ block
        out_ref[place, rows // 16 * 16 :, :] = jnp.zeros((pad - rows // 16 * 16, pad), BF16)
        out_ref[place, :, rows // LANES * LANES :] = jnp.zeros((pad, pad - rows // LANES * LANES), BF16)
        out_ref[place, :rows, :rows] = a_ref[:, block * rows : (block + 1) * rows]


def turned(me_ref, x_ref, *refs):
    tall = refs[-1]
    rows = x_ref.shape[0]
    tall[rows:, :] = jnp.zeros_like(tall[rows:, :])
    tall[:rows, :] = x_ref[...].astype(F32)
    flat = tall[...].T.astype(BF16)
    first = 0
    for out_ref in refs[:-1]:
        out_ref[...] = flat[first : first + out_ref.shape[0]]
        first += out_ref.shape[0]


def coupling(levels, reflect_ref, cotangent_ref, out_ref, tall):
    rows = reflect_ref.shape[1]
    pad = tall.shape[0]
    group, part = out_ref.shape[:2]
    level = pl.program_id(0)

    @pl.when(level < levels)
    def _():
        tall[rows // 8 * 8 :, :] = jnp.zeros_like(tall[rows // 8 * 8 :, :])
        tall[:rows, :] = reflect_ref[0, :, 0, :]
        out_ref[...] = tall[...].T.astype(BF16).reshape(group, part, pad)

    @pl.when(level == levels)
    def _():
        cot = cotangent_ref[...].T
        high = cot.astype(BF16)
        low = (cot - high.astype(F32)).astype(BF16)
        tracked = cot.shape[1]
        out_ref[:, :, :tracked] = high.reshape(group, part, tracked)
        out_ref[:, :, tracked : 2 * tracked] = low.reshape(group, part, tracked)


def halved(value_ref, *refs):
    split(refs, value_ref[...])


def forward_most(own_ref, core_ref, far_ref, panel_ref, out_ref):
    near = times_t(own_ref[...], panel_ref[0]) + times_t(core_ref[...], panel_ref[1])
    out_ref[...] = near + times_t(far_ref[...], panel_ref[2])


def forward_last(degree, step_ref, x_ref, most_ref, panel_ref, *refs):
    product = most_ref[...] + times_t(joined(refs[:-1]), panel_ref[3])
    refs[-1][...] = (x_ref[...].astype(F32) + step_ref[0:1, 0:1] / degree * product).astype(BF16)


def forward_end(step_ref, x_ref, most_ref, panel_ref, me_ref, before_ref, *refs):
    out_ref, pile_ref = refs[-2:]
    pieces = refs[:-2]
    diag = pieces[-HALVES:]
    product = most_ref[...] + times_t(joined(diag), panel_ref[3])
    value = (x_ref[...].astype(F32) + step_ref[0:1, 0:1] * product).astype(BF16)
    first = before_ref.shape[0]
    out_ref[:first] = before_ref[...]
    out_ref[first:] = value
    places = pile_ref.shape[0]
    each = places - 1 + HALVES
    row = 0
    for chunk in range(len(pieces) // each):
        group = pieces[chunk * each : (chunk + 1) * each]
        width = group[0].shape[0]
        for place in range(places - 1):
            pile_ref[me_ref[0] ^ place, row : row + width, :] = group[place][...]
        pile_ref[me_ref[0] ^ (places - 1), row : row + width, :] = joined(group[places - 1 :])
        row += width


def columns_from(pile_ref, out_ref):
    places = pile_ref.shape[0]
    rows = out_ref.shape[1] // places
    for block in range(places):
        out_ref[:, block * rows : (block + 1) * rows] = pile_ref[block, :, :rows]


def merge(levels, rows, me_ref, order_ref, w_ref, rc_ref, field_ref, cmap_ref, level_ref, sums_ref, tail_ref, sems):
    group, part, pad = w_ref.shape
    tracked = order_ref.shape[1]
    tail = level_ref.shape[2]
    copies = [
        pltpu.make_async_copy(rc_ref.at[:, :, pl.ds(tail, 2 * tracked)], tail_ref, sems.at[levels])
    ]
    for level in range(levels):
        lanes = pl.ds(level * pad, pad)
        copies.append(
            pltpu.make_async_copy(rc_ref.at[:, :, lanes], level_ref.at[:, :, lanes], sems.at[level])
        )
    for copy in copies:
        copy.start()
    place = lax.broadcasted_iota(jnp.int32, (pad, tracked), 0)
    order = place + lax.rem(me_ref[0] * rows, ORDERS)
    for _ in range(-(-rows // ORDERS)):
        order = jnp.where(order >= ORDERS, order - ORDERS, order)
    order = jnp.where(place < rows, order, -1)
    onehot = jnp.where(order == order_ref[...], 1.0, 0.0).astype(BF16)
    onehot = jnp.concatenate([onehot, onehot], axis=1)
    copies[0].wait()
    cmap_ref[...] = times_t(tail_ref[...].reshape(group * part, 2 * tracked), onehot).reshape(group, part, pad)
    totals = []
    merged = [w_ref[s].astype(F32) for s in range(group)]
    for level in range(levels):
        copies[level + 1].wait()
        sent = [
            level_ref[s, :, level * pad : (level + 1) * pad].astype(F32) * merged[s] for s in range(group)
        ]
        merged = [merged[s] + sent[s ^ 2**level] for s in range(group)]
    lane = lax.broadcasted_iota(jnp.int32, (part, LANES), 1)
    for s in range(group):
        field = merged[s]
        squared = field * field
        power = jnp.sum(squared, axis=1, keepdims=True)
        weighted = jnp.sum(cmap_ref[s] * squared, axis=1, keepdims=True)
        field_ref[s] = field
        totals.append(jnp.where(lane == 0, power, jnp.where(lane == 1, weighted, 0.0)))
    sums_ref[...] = jnp.concatenate(totals, axis=0).T[: sums_ref.shape[0]]


def unmerge(levels, full, scale, field_ref, cmap_ref, rc_ref, s0, s1, s2, s3, out_ref):
    group, part, pad = field_ref.shape
    sums = (s0[...] + s1[...]) + (s2[...] + s3[...])
    sums = jnp.concatenate([sums] * (LANES // sums.shape[0]), axis=0).T
    grad = []
    for s in range(group):
        power = sums[s * part : (s + 1) * part, 0:1]
        weighted = sums[s * part : (s + 1) * part, 1:2]
        inverse = 1.0 / (power / full + 1e-06)
        first = scale * 2.0 * inverse
        second = scale * 2.0 / full * (weighted * inverse * inverse)
        grad.append((first * cmap_ref[s] - second) * field_ref[s])
    for level in range(levels - 1, -1, -1):
        grad = [
            grad[s]
            + rc_ref[s, :, level * pad : (level + 1) * pad].astype(F32) * grad[s ^ 2**level]
            for s in range(group)
        ]
    for s in range(group):
        out_ref[s] = grad[s].astype(BF16)


def columns_of(me_ref, *refs):
    out_ref, pile = refs[-2:]
    places = pile.shape[0]
    rows = out_ref.shape[1] // places
    first = 0
    each = places - 1 + HALVES
    for chunk in range((len(refs) - 2) // each):
        group = refs[chunk * each : (chunk + 1) * each]
        width = group[0].shape[0]
        for place in range(places - 1):
            pile[me_ref[0] ^ place, first : first + width, :] = group[place][...]
        pile[me_ref[0] ^ (places - 1), first : first + width, :] = joined(group[places - 1 :])
        first += width
    for block in range(places):
        out_ref[:, block * rows : (block + 1) * rows] = pile[block, :, :rows]


def backward_first(first, step_ref, whole_ref, panel_ref, scaled_ref, total_ref, *refs):
    width = scaled_ref.shape[0]
    upstream = whole_ref[first : first + width]
    for ref in refs[HALVES:]:
        ref[...] = whole_ref[width:]
    total_ref[...] = upstream.astype(F32)
    scaled = (step_ref[0:1, 0:1] * upstream.astype(F32)).astype(BF16)
    scaled_ref[...] = scaled
    split(refs[:HALVES], times(scaled, panel_ref[3]).astype(BF16))


def backward_next(degree, step_ref, near_ref, core_ref, far_ref, before_ref, panel_ref, scaled_ref, total_ref, *sent):
    upstream = near_ref[...] + core_ref[...].astype(F32) + far_ref[...].astype(F32)
    total_ref[...] = before_ref[...] + upstream
    scaled = (step_ref[0:1, 0:1] / degree * upstream).astype(BF16)
    scaled_ref[...] = scaled
    split(sent, times(scaled, panel_ref[3]).astype(BF16))


def backward_most(scaled_ref, panel_ref, sent_ref, near_ref, most_ref):
    scaled = scaled_ref[...]
    most_ref[...] = times(scaled, panel_ref[2])
    sent_ref[...] = times(scaled, panel_ref[1]).astype(BF16)
    near_ref[...] = times(scaled, panel_ref[0])


def backward_last(most_ref, *refs):
    refs[-1][...] = (most_ref[...] + joined(refs[:-1]).astype(F32)).astype(BF16)


def product_rows(lefts, right, columns):
    left = jnp.concatenate([ref[:, columns] for ref in lefts], axis=0)
    return lax.dot_general(left, right[...], (((0,), (0,)), ((), ())), preferred_element_type=F32)


def outer_early(*refs):
    rights, out_ref = refs[-TAYLOR:-1], refs[-1]
    chunks = (len(refs) - TAYLOR) // len(rights)

    @pl.loop(0, out_ref.shape[0] // LANES)
    def _(tile):
        place = pl.ds(pl.multiple_of(tile * LANES, LANES), LANES)
        values = [
            product_rows(refs[term * chunks : (term + 1) * chunks], right, place)
            for term, right in enumerate(rights)
        ]
        out_ref[place, :] = functools.reduce(jnp.add, values)


def outer(chunks, first, *refs):
    right, early, out_ref = refs[chunks], refs[chunks + 1], refs[-1]
    tile = pl.program_id(0) + first
    place = pl.ds(pl.multiple_of(tile * LANES, LANES), LANES)
    out_ref[:, 0, :] = product_rows(refs[:chunks], right, slice(None)) + early[place, :]


def outer_rows(first, tiles, lefts, right, early, target, rows, full):
    specs = [pl.BlockSpec((left.shape[0], LANES), lambda i: (0, i + first)) for left in lefts]
    args = [*lefts, right, early]
    if target is not None:
        args.append(target)
    return pl.pallas_call(
        functools.partial(outer, len(lefts), first),
        grid=(tiles,),
        out_shape=shape(rows, 1, full),
        in_specs=specs + [WHOLE] * 2 + [pl.BlockSpec(memory_space=pl.ANY)] * (target is not None),
        out_specs=pl.BlockSpec((LANES, 1, full), lambda i: (i + first, 0, 0)),
        input_output_aliases={} if target is None else {len(args) - 1: 0},
        compiler_params=pltpu.CompilerParams(vmem_limit_bytes=16 * 2**20),
        cost_estimate=pl.CostEstimate(flops=0 if target is None else COST, transcendentals=0, bytes_accessed=1),
    )(*args)


def finish(*refs):
    out_ref = refs[-1]
    rows = out_ref.shape[0]
    values = []
    for chunk in range(len(refs) // 4):
        near, total, core, far = (ref[...].astype(F32) for ref in refs[4 * chunk : 4 * chunk + 4])
        values.append((near + total) + (core + far))
    value = jnp.concatenate(values, axis=0).T
    out_ref[:, 0, :] = value[:rows]


def local(operator, incident, reflect, thickness_table, profile, order_index, cotangent):
    rows, full = operator.shape[1:]
    columns = incident.shape[2]
    levels = reflect.shape[1]
    group = 2**levels
    tracked = order_index.shape[0]
    pad = -(-rows // LANES) * LANES
    part = columns // group
    count = range(CHUNKS)
    me = lax.axis_index("row")
    me_arr = me.reshape(1)
    widths = [columns * share // sum(SPLIT) for share in SPLIT]
    blocks = [shape(width, pad, dtype=BF16) for width in widths]
    wides = [shape(width, pad) for width in widths]
    parts = [[shape(width // HALVES, pad, dtype=BF16)] * HALVES for width in widths]

    rc = pl.pallas_call(
        functools.partial(coupling, levels),
        grid=(levels + 1,),
        out_shape=pltpu.HBM((group, part, levels * pad + 2 * tracked), BF16),
        in_specs=[
            pl.BlockSpec((1, rows, 1, columns), lambda i: (jnp.minimum(i, levels - 1), 0, 0, 0)),
            pl.BlockSpec((tracked, columns), lambda i: (0, 0)),
        ],
        out_specs=pl.BlockSpec((group, part, pad), lambda i: (0, 0, i)),
        scratch_shapes=[pltpu.VMEM((pad, columns), F32)],
        compiler_params=pltpu.CompilerParams(vmem_limit_bytes=10 * 2**20),
        cost_estimate=pl.CostEstimate(flops=0, transcendentals=0, bytes_accessed=1),
    )(
        pltpu.with_memory_space_constraint(reflect.transpose(1, 2, 0, 3), pltpu.HBM),
        pltpu.with_memory_space_constraint(cotangent[0], pltpu.HBM),
    )
    x = call(turned, blocks, after(me_arr, rc), incident[0], scratch=[pltpu.VMEM((pad, columns), F32)])
    rc = over_cuts(rc)
    fars = [over_row(value, 2) for value in x]
    cores = [over_row(value, 1) for value in x]
    panel, step = call(
        operator_blocks,
        (shape(4, pad, pad, dtype=BF16), shape(8, LANES)),
        after(me_arr, x[0]), profile, thickness_table, operator[0],
        limit=12,
    )
    token = panel

    current = list(x)
    stored = [[] for _ in count]
    rights = []
    x = list(x)

    def write_columns(place, pieces, hbm=True):
        return call(
            columns_of,
            (pltpu.HBM if hbm else jax.ShapeDtypeStruct)((columns, full), BF16),
            place, *pieces,
            scratch=[pltpu.VMEM((4, columns, pad), BF16)],
            limit=6,
        )

    for degree in range(TAYLOR, 0, -1):
        next_fars, next_cores = [], []
        for chunk in count:
            far = after(fars[chunk], token)
            halves = call(halved, parts[chunk], far)
            most = call(
                forward_most, wides[chunk], current[chunk], after(cores[chunk], halves[0]), far, panel
            )
            diag = [over_row(half, 1) for half in halves]
            stored[chunk].append((current[chunk], cores[chunk], far, *diag))
            if degree == 1 and chunk == CHUNKS - 1:
                value, pile = call(
                    forward_end,
                    (pltpu.HBM((columns, pad), BF16), pltpu.HBM((4, columns, pad), BF16)),
                    step, x[chunk], most, panel, me_arr, current[0],
                    *[piece for each in count for piece in stored[each][-1]],
                )
            else:
                value = call(
                    functools.partial(forward_last, degree),
                    blocks[chunk], step, x[chunk], most, panel, *diag,
                )
            current[chunk] = value
            token = value
            if degree > 1:
                next_fars.append(over_row(value, 2))
                next_cores.append(over_row(value, 1))
        fars, cores = next_fars, next_cores
        pieces = [piece for chunk in count for piece in stored[chunk][-1]]
        place = after(me_arr, token)
        if degree > 1:
            token = write_columns(place, pieces)
            rights.append(token)

    current[-1], rc = lax.optimization_barrier((current[-1], rc))
    swapped = over_cuts(current[-1].reshape(group, part, pad))
    field, cmap, coupled, sums = pl.pallas_call(
        functools.partial(merge, levels, rows),
        out_shape=(
            shape(group, part, pad),
            shape(group, part, pad),
            shape(group, part, levels * pad, dtype=BF16),
            shape(8, group * part),
        ),
        in_specs=[SCALAR, WHOLE, WHOLE, ANY],
        out_specs=(WHOLE,) * 4,
        scratch_shapes=[
            pltpu.VMEM((group, part, 2 * tracked), BF16),
            pltpu.SemaphoreType.DMA((levels + 1,)),
        ],
        compiler_params=pltpu.CompilerParams(vmem_limit_bytes=12 * 2**20),
        cost_estimate=pl.CostEstimate(flops=0, transcendentals=0, bytes_accessed=1),
    )(
        me_arr,
        order_index.reshape(1, tracked),
        swapped,
        pltpu.with_memory_space_constraint(rc, pltpu.HBM),
    )
    s1, s2, s3 = (over_row(sums, mask) for mask in (1, 2, 3))
    grad = call(
        functools.partial(unmerge, levels, full, 1.0 / math.sqrt(columns)),
        pltpu.HBM((group, part, pad), BF16),
        field, cmap, coupled, sums, s1, s2, s3,
    )
    whole = over_cuts(grad).reshape(columns, pad)
    token = whole

    total = [None] * CHUNKS
    pending = [None] * CHUNKS
    scaled_all = []
    for degree in range(1, TAYLOR + 1):
        for chunk in count:
            outs = [blocks[chunk], wides[chunk]] + parts[chunk]
            if degree == 1:
                scaled, total[chunk], *sent = call(
                    functools.partial(backward_first, 0),
                    outs + ([blocks[1]] if chunk == 0 and CHUNKS == 2 else []),
                    step, after(whole, token), panel,
                )
                if chunk == 0 and CHUNKS == 2:
                    whole = sent.pop()
            else:
                near, core, far = pending[chunk]
                scaled, total[chunk], *sent = call(
                    functools.partial(backward_next, degree), outs,
                    step, near, core, after(far, token), total[chunk], panel,
                )
            scaled_all.append(scaled)
            diag = [over_row(half, 1) for half in sent]
            sent, near, most = call(
                backward_most, [blocks[chunk], wides[chunk], wides[chunk]], after(scaled, sent[0]), panel
            )
            core = over_row(sent, 1)
            sent = call(backward_last, blocks[chunk], most, *diag)
            far = over_row(sent, 2)
            token = sent
            pending[chunk] = (near, core, far)
            if degree == 1 and chunk == CHUNKS - 1:
                token = call(columns_from, shape(columns, full, dtype=BF16), after(pile, token))
                rights.append(token)
            if degree == TAYLOR - 1 and chunk == CHUNKS - 1:
                early = call(
                    outer_early,
                    shape(pad, full),
                    *scaled_all[:-1], after(scaled_all[-1], token), *rights[:0:-1],
                    limit=12,
                )
                token = early
    lefts = [*scaled_all[-CHUNKS:-1], after(scaled_all[-1], token)]
    tiles = -(-rows // LANES)
    top = tiles * 3 // 5
    grad_matrix = outer_rows(0, top, lefts, rights[0], early, None, rows, full)
    for late in pending[:-1]:
        grad_matrix = after(grad_matrix, late[2])
    grad_matrix = outer_rows(top, tiles - top, lefts, rights[0], early, grad_matrix, rows, full)
    args = []
    for chunk in count:
        near, core, far = pending[chunk]
        args += [near, total[chunk], core, far]
    args[-1] = after(args[-1], grad_matrix)
    grad_incident = call(finish, shape(rows, 1, columns), *args)
    return (grad_matrix.transpose(1, 0, 2), grad_incident.transpose(1, 0, 2))


def solution(mesh):
    return jax.shard_map(
        local,
        mesh=mesh,
        in_specs=(
            P("cuts", "row", None),
            P("cuts", "row", None),
            P("cuts", None, "row", None),
            P(),
            P("cuts"),
            P(),
            P("cuts", None, None),
        ),
        out_specs=(P("cuts", "row", None), P("cuts", "row", None)),
        check_vma=False,
    )
```
